256 devices in a mesh: rep: 4 (over x_lo, core), shard: 64 (over z, y, x_hi).
Axes of the slice: x: 4 (x_hi: 2, x_lo: 2; x = x_hi * 2 + x_lo), y: 4, z: 8, core: 2. Of those that a mesh axis runs over, the one named last changes fastest.
Arguments:
- grad: float32 [128, 512, 512], P('rep', 'shard'), may hold values from -60 to 60
- momentum: bfloat16 [128, 512, 512], P('rep', 'shard'), may hold values from -6 to 6
- owners: int32 [128, 1], P('rep'), may hold values from 0 to 63, as said below
- left_roots: bfloat16 [4, 64, 2, 512, 512], P('rep', 'shard'), may hold values from -1 to 2
- right_roots: bfloat16 [4, 64, 2, 512, 512], P('rep', 'shard'), may hold values from -1 to 2
Outputs:
- momentum_next: bfloat16 [128, 512, 512], P('rep', 'shard')
- update: bfloat16 [128, 512, 512], P(None, 'shard')
The draws below stay inside these ranges and needn't reach their ends.
Inputs may be any that keep to these rules, and one draw needn't show every extreme that they name: `owners`: within the 32 blocks of each replica part no owner is named more than 2 times, and some owner exactly 2 times.
All inputs are finite; a program needn't handle non-finite values.
Results may differ from the reference program's by a relative error of at most 0.0059.
Values may be sent and summed in bfloat16 or wider, within the bound.
No kernel may reach another device: no remote copies, remote signals or barrier semaphores. Data moves between devices by JAX's collectives and lax.ppermute only.
A program may use at most 64 MiB of HBM per device.

```python
import math
import jax
import jax.numpy as jnp
from jax import lax

B = 512
CAP = 2
NBR = 32
BLOCKS = 128
N_REP = 4
N_SHARD = 64


def draw_grad(key, part):
    key = jax.random.fold_in(key, 11)
    keys = jax.random.split(key, 3)
    row_scale = jnp.exp(jax.random.uniform(keys[1], (BLOCKS, B, 1), jnp.float32, math.log(0.3), math.log(3.0)))
    col_scale = jnp.exp(jax.random.uniform(keys[2], (BLOCKS, 1, B), jnp.float32, math.log(0.3), math.log(3.0)))
    noise = jax.random.truncated_normal(keys[0], -6.0, 6.0, (BLOCKS, B, B), jnp.float32)
    values = noise * row_scale * col_scale
    return values.astype(jnp.float32)


def root_factor(key, lowest, highest, spread):
    keys = jax.random.split(key, 2)
    shape = (N_REP, N_SHARD, CAP, B, B)
    diagonal = jnp.exp(jax.random.uniform(keys[0], (N_REP, N_SHARD, CAP, B, 1), jnp.float32, math.log(lowest), math.log(highest)))
    noise = jax.random.truncated_normal(keys[1], -4.0, 4.0, shape, jnp.float32)
    symmetric = (noise + jnp.swapaxes(noise, -1, -2)) * (spread / math.sqrt(2.0 * B))
    rows_index = jax.lax.broadcasted_iota(jnp.int32, (B, B), 0)
    cols_index = jax.lax.broadcasted_iota(jnp.int32, (B, B), 1)
    values = jnp.where(rows_index == cols_index, diagonal, symmetric)
    return values.astype(jnp.bfloat16)


def draw_left_roots(key, part):
    key = jax.random.fold_in(key, 12)
    return root_factor(key, 0.5, 2.0, 0.3)


def draw_right_roots(key, part):
    key = jax.random.fold_in(key, 13)
    return root_factor(key, 0.5, 2.0, 0.3)


def owner_part(key):
    keys = jax.random.split(key, 3)
    total_slots = N_SHARD * CAP
    positions = jnp.arange(total_slots, dtype=jnp.int32)
    scores = jax.random.randint(keys[0], (total_slots,), 0, 1 << 20, dtype=jnp.int32) * total_slots + positions
    scores = jnp.where(positions < CAP, -1 - positions, scores)
    order = jnp.argsort(scores, stable=True).astype(jnp.int32)
    chosen = order[:NBR] // CAP
    relabel = jax.random.permutation(keys[1], N_SHARD).astype(jnp.int32)
    named = relabel[chosen]
    shuffle = jax.random.permutation(keys[2], NBR).astype(jnp.int32)
    return named[shuffle]


def draw_owners(key, part):
    key = jax.random.fold_in(key, 14)
    keys = jax.random.split(key, N_REP)
    parts_drawn = jax.vmap(owner_part)(keys)
    return parts_drawn.reshape(BLOCKS, 1).astype(jnp.int32)


def steps_of(stream_key, shape, cuts, least, high):
    def one(axis_at, blocks):
        draws = jax.random.uniform(jax.random.fold_in(jax.random.fold_in(stream_key, 6), axis_at), (blocks,), jnp.float32, least / len(cuts), high / len(cuts))
        return jnp.repeat(jnp.exp(draws), shape[axis_at] // blocks).reshape((-1,) + (1,) * (len(shape) - axis_at - 1))

    gain = one(*cuts[0])
    for cut in cuts[1:]:
        gain = gain * one(*cut)
    return gain


def scatter_about(key, shape, scale, most, cuts=(), held_as=jnp.bfloat16):
    result = scale * jax.random.normal(key, shape, jnp.float32)
    if cuts:
        result = result * steps_of(key, shape, cuts, -0.22, 0.18)
    return jnp.clip(result, -most, most).astype(held_as)


def setup_inputs(seed: int = 0) -> dict:
    splits = jax.random.split(jax.random.key(seed), 6)
    grad = draw_grad(jax.random.fold_in(splits[5], 71), 0)
    momentum = scatter_about(splits[1], (BLOCKS, B, B), 1.0, 6.0, ((0, 4), (1, 64)))
    owners = draw_owners(jax.random.fold_in(splits[5], 71), 0)
    left_roots = draw_left_roots(jax.random.fold_in(splits[5], 71), 0)
    right_roots = draw_right_roots(jax.random.fold_in(splits[5], 71), 0)
    return dict(grad=grad, momentum=momentum, owners=owners, left_roots=left_roots, right_roots=right_roots)


momentum_decay = 0.9
graft_eps = 1e-06

def slot_numbers(owner_ids):
    count = owner_ids.shape[-1]
    current = lax.broadcasted_iota(jnp.int32, (count, count), 0)
    previous = lax.broadcasted_iota(jnp.int32, (count, count), 1)
    before = previous < current
    same_owner = owner_ids[..., :, None] == owner_ids[..., None, :]
    return lax.optimization_barrier(jnp.sum((same_owner & before).astype(jnp.int32), axis=-1)).astype(jnp.int32)

def precondition(gradient_block, left_root, right_root):
    half_product = jnp.dot(left_root, gradient_block.astype(jnp.bfloat16), preferred_element_type=jnp.float32).astype(jnp.bfloat16)
    precond = jnp.dot(half_product, right_root, preferred_element_type=jnp.float32)
    grad_norm = jnp.sqrt(jnp.sum(gradient_block * gradient_block))
    pre_norm = jnp.sqrt(jnp.sum(precond * precond) + graft_eps)
    return precond * (grad_norm / pre_norm)

def reference(grad, momentum, owners, left_roots, right_roots):
    owner_parts = owners.reshape(N_REP, NBR).astype(jnp.int32)
    slots = slot_numbers(owner_parts)
    part_ids = lax.broadcasted_iota(jnp.int32, (N_REP, NBR), 0)
    flat_index = ((part_ids * N_SHARD + owner_parts) * CAP + slots).reshape(BLOCKS).astype(jnp.int32)
    left_flat = left_roots.reshape(N_REP * N_SHARD * CAP, B, B)
    right_flat = right_roots.reshape(N_REP * N_SHARD * CAP, B, B)

    def one_block(item):
        gradient_block, where_slot = item
        left_root = lax.dynamic_index_in_dim(left_flat, where_slot, 0, keepdims=False)
        right_root = lax.dynamic_index_in_dim(right_flat, where_slot, 0, keepdims=False)
        return precondition(gradient_block, left_root, right_root)
    grafted = lax.map(one_block, (grad, flat_index))
    momentum_next = (momentum_decay * momentum.astype(jnp.float32) + grafted).astype(jnp.bfloat16)
    stored = lax.optimization_barrier(momentum_next)
    update = (grafted + momentum_decay * stored.astype(jnp.float32)).astype(jnp.bfloat16)
    return (momentum_next, update)
```

```python
import jax
import jax.numpy as jnp
from jax import lax
from jax.experimental import pallas as pl
from jax.experimental.pallas import tpu as pltpu
from jax.sharding import PartitionSpec as P

momentum_decay = 0.9
graft_eps = 1e-06
LANES = 128


def pack_kernel(owner_ref, grad_ref, out_ref, index_ref, count_ref):
    owners, capacity = count_ref.shape[0], out_ref.shape[0] // count_ref.shape[0]
    blocks, _, width = grad_ref.shape
    out_ref[...] = jnp.zeros_like(out_ref)

    def clear(at, carry):
        count_ref[at] = 0
        return carry

    lax.fori_loop(0, owners, clear, 0, unroll=8)

    def place(block, carry):
        owner = owner_ref[block, 0]
        slot = count_ref[owner]
        count_ref[owner] = slot + 1
        index = owner * capacity + slot
        index_ref[block] = index
        rows = grad_ref[block]
        stacked = jnp.concatenate(
            [rows[:, at : at + LANES] for at in range(0, width, LANES)], axis=0
        )
        out_ref[index] = stacked.astype(out_ref.dtype)
        return carry

    lax.fori_loop(0, blocks, place, 0, unroll=4)


def pack(grad, owners, shard_count, capacity):
    blocks, rows, width = grad.shape
    stacked_rows = rows * (width // LANES)
    return pl.pallas_call(
        pack_kernel,
        out_shape=(
            jax.ShapeDtypeStruct((shard_count * capacity, stacked_rows, LANES), jnp.bfloat16),
            jax.ShapeDtypeStruct((blocks,), jnp.int32),
        ),
        in_specs=[
            pl.BlockSpec(memory_space=pltpu.SMEM),
            pl.BlockSpec(memory_space=pltpu.VMEM),
        ],
        out_specs=(
            pl.BlockSpec(memory_space=pltpu.VMEM),
            pl.BlockSpec(memory_space=pltpu.SMEM),
        ),
        scratch_shapes=[pltpu.SMEM((shard_count,), jnp.int32)],
        compiler_params=pltpu.CompilerParams(vmem_limit_bytes=16 * 1024 * 1024),
    )(owners, grad)


def precondition_kernel(arrived_ref, left_ref, right_ref, out_ref):
    shards, slot_rows, _ = arrived_ref.shape
    capacity, order, _ = left_ref.shape
    stacked = slot_rows // capacity
    rows = order // shards
    for slot in range(capacity):
        pieces = arrived_ref[:, slot * stacked : (slot + 1) * stacked, :].astype(jnp.float32)
        block = jnp.concatenate(
            [
                pieces[:, at : at + rows, :].reshape(order, LANES)
                for at in range(0, stacked, rows)
            ],
            axis=1,
        )
        grad_norm = jnp.sqrt(jnp.sum(block * block))
        half = jnp.dot(
            left_ref[slot], block.astype(jnp.bfloat16), preferred_element_type=jnp.float32
        ).astype(jnp.bfloat16)
        precond = jnp.dot(half, right_ref[slot], preferred_element_type=jnp.float32)
        pre_norm = jnp.sqrt(jnp.sum(precond * precond) + graft_eps)
        grafted = precond * (grad_norm / pre_norm)
        out = jnp.concatenate(
            [
                grafted[:, at : at + LANES].reshape(shards, rows, LANES)
                for at in range(0, order, LANES)
            ],
            axis=1,
        )
        out_ref[:, slot * stacked : (slot + 1) * stacked, :] = out.astype(out_ref.dtype)


def precondition(arrived, left_root, right_root):
    return pl.pallas_call(
        precondition_kernel,
        out_shape=jax.ShapeDtypeStruct(arrived.shape, jnp.bfloat16),
        compiler_params=pltpu.CompilerParams(vmem_limit_bytes=40 * 1024 * 1024),
    )(arrived, left_root, right_root)


def step_kernel(index_ref, returned_ref, momentum_ref, next_ref, update_ref):
    blocks, rows, width = momentum_ref.shape

    def one(block, carry):
        stacked = returned_ref[index_ref[block]].astype(jnp.float32)
        grafted = jnp.concatenate(
            [stacked[at : at + rows] for at in range(0, stacked.shape[0], rows)], axis=1
        )
        momentum_next = (
            momentum_decay * momentum_ref[block].astype(jnp.float32) + grafted
        ).astype(jnp.bfloat16)
        next_ref[block] = momentum_next
        update_ref[block] = (
            grafted + momentum_decay * momentum_next.astype(jnp.float32)
        ).astype(jnp.bfloat16)
        return carry

    lax.fori_loop(0, blocks, one, 0, unroll=4)


def step(index, returned, momentum):
    return pl.pallas_call(
        step_kernel,
        out_shape=(
            jax.ShapeDtypeStruct(momentum.shape, jnp.bfloat16),
            jax.ShapeDtypeStruct(momentum.shape, jnp.bfloat16),
        ),
        in_specs=[
            pl.BlockSpec(memory_space=pltpu.SMEM),
            pl.BlockSpec(memory_space=pltpu.VMEM),
            pl.BlockSpec(memory_space=pltpu.VMEM),
        ],
        compiler_params=pltpu.CompilerParams(vmem_limit_bytes=16 * 1024 * 1024),
    )(index, returned, momentum)


def assemble_kernel(place_ref, own_ref, core_ref, chip_ref, cross_ref, out_ref, sems):
    copies = []
    for at, piece in enumerate((own_ref, core_ref, chip_ref, cross_ref)):
        copies.append(pltpu.make_async_copy(piece, out_ref.at[place_ref[at]], sems.at[at]))
    for copy in copies:
        copy.start()
    for copy in copies:
        copy.wait()


def assemble(places, pieces):
    shape = pieces[0].shape
    return pl.pallas_call(
        assemble_kernel,
        out_shape=jax.ShapeDtypeStruct((len(pieces),) + shape, pieces[0].dtype),
        in_specs=[pl.BlockSpec(memory_space=pltpu.SMEM)]
        + [pl.BlockSpec(memory_space=pl.ANY)] * len(pieces),
        out_specs=pl.BlockSpec(memory_space=pl.ANY),
        scratch_shapes=[pltpu.SemaphoreType.DMA((len(pieces),))],
    )(places, *pieces)


def gather_parts(update_rows):
    swap_core = [(at, at ^ 1) for at in range(4)]
    swap_chip = [(at, at ^ 2) for at in range(4)]
    chip = lax.ppermute(update_rows, "rep", swap_chip)
    core = lax.ppermute(update_rows, "rep", swap_core)
    cross = lax.ppermute(chip, "rep", swap_core)
    places = lax.axis_index("rep") ^ jnp.arange(4, dtype=jnp.int32)
    out = assemble(places, (update_rows, core, chip, cross))
    return out.reshape((-1,) + update_rows.shape[1:])


def local(grad, momentum, owners, left_roots, right_roots):
    shard_count = lax.axis_size("shard")
    capacity = left_roots.shape[2]
    outgoing, index = pack(grad, owners, shard_count, capacity)
    stacked = outgoing.shape[1]
    outgoing = outgoing.reshape(shard_count, capacity * stacked, LANES)
    arrived = lax.all_to_all(outgoing, "shard", 0, 0, tiled=True)
    grafted = precondition(arrived, left_roots[0, 0], right_roots[0, 0])
    returned = lax.all_to_all(grafted, "shard", 0, 0, tiled=True)
    returned = returned.reshape(shard_count * capacity, stacked, LANES)
    momentum_next, update_rows = step(index, returned, momentum)
    return momentum_next, gather_parts(update_rows)


def solution(mesh):
    placed = (
        P("rep", "shard", None),
        P("rep", "shard", None),
        P("rep", None),
        P("rep", "shard", None, None, None),
        P("rep", "shard", None, None, None),
    )
    return jax.shard_map(
        local,
        mesh=mesh,
        in_specs=placed,
        out_specs=(P("rep", "shard", None), P(None, "shard", None)),
        check_vma=False,
    )
```

```python
import jax
import jax.numpy as jnp
from jax import lax
from jax.experimental import pallas as pl
from jax.experimental.pallas import tpu as pltpu
from jax.sharding import PartitionSpec as P

momentum_decay = 0.9
graft_eps = 1e-06
LANES = 128


def pack_kernel(owner_ref, grad_ref, out_ref, index_ref, count_ref):
    owners, capacity = count_ref.shape[0], out_ref.shape[0] // count_ref.shape[0]
    blocks, _, width = grad_ref.shape
    out_ref[...] = jnp.zeros_like(out_ref)

    def clear(at, carry):
        count_ref[at] = 0
        return carry

    lax.fori_loop(0, owners, clear, 0, unroll=8)

    def place(block, carry):
        owner = owner_ref[block, 0]
        slot = count_ref[owner]
        count_ref[owner] = slot + 1
        index = owner * capacity + slot
        index_ref[block] = index
        rows = grad_ref[block]
        stacked = jnp.concatenate(
            [rows[:, at : at + LANES] for at in range(0, width, LANES)], axis=0
        )
        out_ref[index] = stacked.astype(out_ref.dtype)
        return carry

    lax.fori_loop(0, blocks, place, 0, unroll=4)


def pack(grad, owners, shard_count, capacity):
    blocks, rows, width = grad.shape
    stacked_rows = rows * (width // LANES)
    return pl.pallas_call(
        pack_kernel,
        out_shape=(
            jax.ShapeDtypeStruct((shard_count * capacity, stacked_rows, LANES), jnp.bfloat16),
            jax.ShapeDtypeStruct((blocks,), jnp.int32),
        ),
        in_specs=[
            pl.BlockSpec(memory_space=pltpu.SMEM),
            pl.BlockSpec(memory_space=pltpu.VMEM),
        ],
        out_specs=(
            pl.BlockSpec(memory_space=pltpu.VMEM),
            pl.BlockSpec(memory_space=pltpu.SMEM),
        ),
        scratch_shapes=[pltpu.SMEM((shard_count,), jnp.int32)],
        compiler_params=pltpu.CompilerParams(vmem_limit_bytes=16 * 1024 * 1024),
    )(owners, grad)


def precondition_kernel(arrived_ref, left_ref, right_ref, out_ref):
    shards, slot_rows, _ = arrived_ref.shape
    capacity, order, _ = left_ref.shape
    stacked = slot_rows // capacity
    rows = order // shards
    for slot in range(capacity):
        pieces = arrived_ref[:, slot * stacked : (slot + 1) * stacked, :].astype(jnp.float32)
        block = jnp.concatenate(
            [
                pieces[:, at : at + rows, :].reshape(order, LANES)
                for at in range(0, stacked, rows)
            ],
            axis=1,
        )
        grad_norm = jnp.sqrt(jnp.sum(block * block))
        half = jnp.dot(
            left_ref[slot], block.astype(jnp.bfloat16), preferred_element_type=jnp.float32
        ).astype(jnp.bfloat16)
        precond = jnp.dot(half, right_ref[slot], preferred_element_type=jnp.float32)
        pre_norm = jnp.sqrt(jnp.sum(precond * precond) + graft_eps)
        grafted = precond * (grad_norm / pre_norm)
        out = jnp.concatenate(
            [
                grafted[:, at : at + LANES].reshape(shards, rows, LANES)
                for at in range(0, order, LANES)
            ],
            axis=1,
        )
        out_ref[:, slot * stacked : (slot + 1) * stacked, :] = out.astype(out_ref.dtype)


def precondition(arrived, left_root, right_root):
    return pl.pallas_call(
        precondition_kernel,
        out_shape=jax.ShapeDtypeStruct(arrived.shape, jnp.bfloat16),
        compiler_params=pltpu.CompilerParams(vmem_limit_bytes=40 * 1024 * 1024),
    )(arrived, left_root, right_root)


def step_kernel(index_ref, returned_ref, momentum_ref, next_ref, update_ref):
    blocks, rows, width = momentum_ref.shape

    def one(block, carry):
        stacked = returned_ref[index_ref[block]].astype(jnp.float32)
        grafted = jnp.concatenate(
            [stacked[at : at + rows] for at in range(0, stacked.shape[0], rows)], axis=1
        )
        momentum_next = (
            momentum_decay * momentum_ref[block].astype(jnp.float32) + grafted
        ).astype(jnp.bfloat16)
        next_ref[block] = momentum_next
        update_ref[block] = (
            grafted + momentum_decay * momentum_next.astype(jnp.float32)
        ).astype(jnp.bfloat16)
        return carry

    lax.fori_loop(0, blocks, one, 0, unroll=4)


def step(index, returned, momentum):
    return pl.pallas_call(
        step_kernel,
        out_shape=(
            jax.ShapeDtypeStruct(momentum.shape, jnp.bfloat16),
            jax.ShapeDtypeStruct(momentum.shape, jnp.bfloat16),
        ),
        in_specs=[
            pl.BlockSpec(memory_space=pltpu.SMEM),
            pl.BlockSpec(memory_space=pltpu.VMEM),
            pl.BlockSpec(memory_space=pltpu.VMEM),
        ],
        compiler_params=pltpu.CompilerParams(vmem_limit_bytes=16 * 1024 * 1024),
    )(index, returned, momentum)


def assemble_kernel(place_ref, own_ref, core_ref, chip_ref, cross_ref, out_ref, sems):
    copies = []
    for at, piece in enumerate((own_ref, core_ref, chip_ref, cross_ref)):
        copies.append(pltpu.make_async_copy(piece, out_ref.at[place_ref[at]], sems.at[at]))
    for copy in copies:
        copy.start()
    for copy in copies:
        copy.wait()


def assemble(places, pieces):
    shape = pieces[0].shape
    return pl.pallas_call(
        assemble_kernel,
        out_shape=jax.ShapeDtypeStruct((len(pieces),) + shape, pieces[0].dtype),
        in_specs=[pl.BlockSpec(memory_space=pltpu.SMEM)]
        + [pl.BlockSpec(memory_space=pltpu.VMEM)] * len(pieces),
        out_specs=pl.BlockSpec(memory_space=pl.ANY),
        scratch_shapes=[pltpu.SemaphoreType.DMA((len(pieces),))],
    )(places, *pieces)


def gather_parts(update_rows):
    swap_core = [(at, at ^ 1) for at in range(4)]
    swap_chip = [(at, at ^ 2) for at in range(4)]
    chip = lax.ppermute(update_rows, "rep", swap_chip)
    core = lax.ppermute(update_rows, "rep", swap_core)
    cross = lax.ppermute(chip, "rep", swap_core)
    places = lax.axis_index("rep") ^ jnp.arange(4, dtype=jnp.int32)
    out = assemble(places, (update_rows, core, chip, cross))
    return out.reshape((-1,) + update_rows.shape[1:])


def local(grad, momentum, owners, left_roots, right_roots):
    shard_count = lax.axis_size("shard")
    capacity = left_roots.shape[2]
    outgoing, index = pack(grad, owners, shard_count, capacity)
    stacked = outgoing.shape[1]
    outgoing = outgoing.reshape(shard_count, capacity * stacked, LANES)
    arrived = lax.all_to_all(outgoing, "shard", 0, 0, tiled=True)
    grafted = precondition(arrived, left_roots[0, 0], right_roots[0, 0])
    returned = lax.all_to_all(grafted, "shard", 0, 0, tiled=True)
    returned = returned.reshape(shard_count * capacity, stacked, LANES)
    momentum_next, update_rows = step(index, returned, momentum)
    return momentum_next, gather_parts(update_rows)


def solution(mesh):
    placed = (
        P("rep", "shard", None),
        P("rep", "shard", None),
        P("rep", None),
        P("rep", "shard", None, None, None),
        P("rep", "shard", None, None, None),
    )
    return jax.shard_map(
        local,
        mesh=mesh,
        in_specs=placed,
        out_specs=(P("rep", "shard", None), P(None, "shard", None)),
        check_vma=False,
    )
```

```python
import jax
import jax.numpy as jnp
from jax import lax
from jax.experimental import pallas as pl
from jax.experimental.pallas import tpu as pltpu
from jax.sharding import PartitionSpec as P

momentum_decay = 0.9
graft_eps = 1e-06
LANES = 128
HOPS = (36, 8)


def pack_kernel(owner_ref, token_ref, grad_ref, out_ref, index_ref, count_ref):
    owners, capacity = count_ref.shape[0], out_ref.shape[0] // count_ref.shape[0]
    blocks, _, width = grad_ref.shape
    late = lax.rem(lax.axis_index("rep"), 2) == 1
    out_ref[...] = jnp.zeros_like(out_ref)

    def clear(at, carry):
        count_ref[at] = 0
        return carry

    lax.fori_loop(0, owners, clear, 0, unroll=16)

    def place(block, carry):
        owner = jnp.where(late, token_ref[0, block], owner_ref[0, block])
        slot = count_ref[owner]
        count_ref[owner] = slot + 1
        index = owner * capacity + slot
        index_ref[block] = index
        rows = grad_ref[block]
        stacked = jnp.concatenate(
            [rows[:, at : at + LANES] for at in range(0, width, LANES)], axis=0
        )
        out_ref[index] = stacked.astype(out_ref.dtype)
        return carry

    lax.fori_loop(0, blocks, place, 0, unroll=8)


def pack(grad, owners, token, shard_count, capacity):
    blocks, rows, width = grad.shape
    stacked_rows = rows * (width // LANES)
    return pl.pallas_call(
        pack_kernel,
        out_shape=(
            jax.ShapeDtypeStruct((shard_count * capacity, stacked_rows, LANES), jnp.bfloat16),
            jax.ShapeDtypeStruct((blocks,), jnp.int32),
        ),
        in_specs=[
            pl.BlockSpec(memory_space=pltpu.SMEM),
            pl.BlockSpec(memory_space=pltpu.SMEM),
            pl.BlockSpec(memory_space=pltpu.VMEM),
        ],
        out_specs=(
            pl.BlockSpec(memory_space=pltpu.VMEM),
            pl.BlockSpec(memory_space=pltpu.SMEM),
        ),
        scratch_shapes=[pltpu.SMEM((shard_count,), jnp.int32)],
        compiler_params=pltpu.CompilerParams(vmem_limit_bytes=16 * 1024 * 1024),
    )(owners, token, grad)


def precondition_kernel(arrived_ref, left_ref, right_ref, out_ref):
    shards, slot_rows, _ = arrived_ref.shape
    capacity, order, _ = left_ref.shape
    stacked = slot_rows // capacity
    rows = order // shards
    for slot in range(capacity):
        pieces = arrived_ref[:, slot * stacked : (slot + 1) * stacked, :].astype(jnp.float32)
        block = jnp.concatenate(
            [
                pieces[:, at : at + rows, :].reshape(order, LANES)
                for at in range(0, stacked, rows)
            ],
            axis=1,
        )
        grad_norm = jnp.sqrt(jnp.sum(block * block))
        half = jnp.dot(
            left_ref[slot], block.astype(jnp.bfloat16), preferred_element_type=jnp.float32
        ).astype(jnp.bfloat16)
        precond = jnp.dot(half, right_ref[slot], preferred_element_type=jnp.float32)
        pre_norm = jnp.sqrt(jnp.sum(precond * precond) + graft_eps)
        grafted = precond * (grad_norm / pre_norm)
        out = jnp.concatenate(
            [
                grafted[:, at : at + LANES].reshape(shards, rows, LANES)
                for at in range(0, order, LANES)
            ],
            axis=1,
        )
        out_ref[:, slot * stacked : (slot + 1) * stacked, :] = out.astype(out_ref.dtype)


def precondition(arrived, left_root, right_root):
    return pl.pallas_call(
        precondition_kernel,
        out_shape=jax.ShapeDtypeStruct(arrived.shape, jnp.bfloat16),
        compiler_params=pltpu.CompilerParams(vmem_limit_bytes=40 * 1024 * 1024),
    )(arrived, left_root, right_root)


def step_kernel(index_ref, returned_ref, momentum_ref, next_ref, update_ref):
    blocks, rows, width = momentum_ref.shape

    def one(block, carry):
        stacked = returned_ref[index_ref[block]].astype(jnp.float32)
        grafted = jnp.concatenate(
            [stacked[at : at + rows] for at in range(0, stacked.shape[0], rows)], axis=1
        )
        momentum_next = (
            momentum_decay * momentum_ref[block].astype(jnp.float32) + grafted
        ).astype(jnp.bfloat16)
        next_ref[block] = momentum_next
        update_ref[block] = (
            grafted + momentum_decay * momentum_next.astype(jnp.float32)
        ).astype(jnp.bfloat16)
        return carry

    lax.fori_loop(0, blocks, one, 0, unroll=4)


def step(index, returned, momentum):
    return pl.pallas_call(
        step_kernel,
        out_shape=(
            jax.ShapeDtypeStruct(momentum.shape, jnp.bfloat16),
            jax.ShapeDtypeStruct(momentum.shape, jnp.bfloat16),
        ),
        in_specs=[
            pl.BlockSpec(memory_space=pltpu.SMEM),
            pl.BlockSpec(memory_space=pltpu.VMEM),
            pl.BlockSpec(memory_space=pltpu.VMEM),
        ],
        compiler_params=pltpu.CompilerParams(vmem_limit_bytes=16 * 1024 * 1024),
    )(index, returned, momentum)


def assemble_kernel(place_ref, own_ref, core_ref, chip_ref, cross_ref, out_ref, sems):
    copies = []
    for at, piece in enumerate((own_ref, core_ref, chip_ref, cross_ref)):
        copies.append(pltpu.make_async_copy(piece, out_ref.at[place_ref[at]], sems.at[at]))
    for copy in copies:
        copy.start()
    for copy in copies:
        copy.wait()


def assemble(places, pieces):
    shape = pieces[0].shape
    return pl.pallas_call(
        assemble_kernel,
        out_shape=jax.ShapeDtypeStruct((len(pieces),) + shape, pieces[0].dtype),
        in_specs=[pl.BlockSpec(memory_space=pltpu.SMEM)]
        + [pl.BlockSpec(memory_space=pltpu.VMEM)] * len(pieces),
        out_specs=pl.BlockSpec(memory_space=pl.ANY),
        scratch_shapes=[pltpu.SemaphoreType.DMA((len(pieces),))],
        compiler_params=pltpu.CompilerParams(vmem_limit_bytes=8 * 1024 * 1024),
    )(places, *pieces)


def gather_parts(update_rows):
    swap_core = [(at, at ^ 1) for at in range(4)]
    swap_chip = [(at, at ^ 2) for at in range(4)]
    chip = lax.ppermute(update_rows, "rep", swap_chip)
    core = lax.ppermute(update_rows, "rep", swap_core)
    cross = lax.ppermute(chip, "rep", swap_core)
    places = lax.axis_index("rep") ^ jnp.arange(4, dtype=jnp.int32)
    out = assemble(places, (update_rows, core, chip, cross))
    return out.reshape((-1,) + update_rows.shape[1:])


def hand_along(owners):
    shards = lax.axis_size("shard")
    for distance in HOPS:
        hops = [
            (part * shards + at, part * shards + (at + distance) % shards)
            for part in range(1, lax.axis_size("rep"), 2)
            for at in range(shards)
        ]
        owners = lax.ppermute(owners, ("rep", "shard"), hops)
    return owners


def local(grad, momentum, owners, left_roots, right_roots):
    shard_count = lax.axis_size("shard")
    capacity = left_roots.shape[2]
    owners = owners.reshape(1, -1)
    outgoing, index = pack(grad, owners, hand_along(owners), shard_count, capacity)
    stacked = outgoing.shape[1]
    outgoing = outgoing.reshape(shard_count, capacity * stacked, LANES)
    arrived = lax.all_to_all(outgoing, "shard", 0, 0, tiled=True)
    grafted = precondition(arrived, left_roots[0, 0], right_roots[0, 0])
    returned = lax.all_to_all(grafted, "shard", 0, 0, tiled=True)
    returned = returned.reshape(shard_count * capacity, stacked, LANES)
    momentum_next, update_rows = step(index, returned, momentum)
    return momentum_next, gather_parts(update_rows)


def solution(mesh):
    placed = (
        P("rep", "shard", None),
        P("rep", "shard", None),
        P("rep", None),
        P("rep", "shard", None, None, None),
        P("rep", "shard", None, None, None),
    )
    return jax.shard_map(
        local,
        mesh=mesh,
        in_specs=placed,
        out_specs=(P("rep", "shard", None), P(None, "shard", None)),
        check_vma=False,
    )
```

```python
import functools

import jax
import jax.numpy as jnp
from jax import lax
from jax.experimental import pallas as pl
from jax.experimental.pallas import tpu as pltpu
from jax.sharding import PartitionSpec as P

momentum_decay = 0.9
graft_eps = 1e-06
LANES = 128
HOPS = (36, 2)


def pack_kernel(owner_ref, token_ref, grad_ref, out_ref, index_ref, count_ref):
    owners, capacity = count_ref.shape[0], out_ref.shape[0] // count_ref.shape[0]
    blocks, _, width = grad_ref.shape
    late = lax.rem(lax.axis_index("rep"), 2) == 1
    out_ref[...] = jnp.zeros_like(out_ref)

    def clear(at, carry):
        count_ref[at] = 0
        return carry

    lax.fori_loop(0, owners, clear, 0, unroll=True)

    def place(block, carry):
        owner = jnp.where(late, token_ref[0, block], owner_ref[0, block])
        slot = count_ref[owner]
        count_ref[owner] = slot + 1
        index = owner * capacity + slot
        index_ref[block] = index
        rows = grad_ref[block]
        stacked = jnp.concatenate(
            [rows[:, at : at + LANES] for at in range(0, width, LANES)], axis=0
        )
        out_ref[index] = stacked.astype(out_ref.dtype)
        return carry

    lax.fori_loop(0, blocks, place, 0, unroll=True)


def pack(grad, owners, token, shard_count, capacity):
    blocks, rows, width = grad.shape
    stacked_rows = rows * (width // LANES)
    return pl.pallas_call(
        pack_kernel,
        out_shape=(
            jax.ShapeDtypeStruct((shard_count * capacity, stacked_rows, LANES), jnp.bfloat16),
            jax.ShapeDtypeStruct((blocks,), jnp.int32),
        ),
        in_specs=[
            pl.BlockSpec(memory_space=pltpu.SMEM),
            pl.BlockSpec(memory_space=pltpu.SMEM),
            pl.BlockSpec(memory_space=pltpu.VMEM),
        ],
        out_specs=(
            pl.BlockSpec(memory_space=pltpu.VMEM),
            pl.BlockSpec(memory_space=pltpu.SMEM),
        ),
        scratch_shapes=[pltpu.SMEM((shard_count,), jnp.int32)],
        compiler_params=pltpu.CompilerParams(vmem_limit_bytes=16 * 1024 * 1024),
    )(owners, token, grad)


def precondition_kernel(arrived_ref, left_ref, right_ref, out_ref):
    shards, slot_rows, _ = arrived_ref.shape
    capacity, order, _ = left_ref.shape
    stacked = slot_rows // capacity
    rows = order // shards
    for slot in range(capacity):
        pieces = arrived_ref[:, slot * stacked : (slot + 1) * stacked, :].astype(jnp.float32)
        block = jnp.concatenate(
            [
                pieces[:, at : at + rows, :].reshape(order, LANES)
                for at in range(0, stacked, rows)
            ],
            axis=1,
        )
        grad_norm = jnp.sqrt(jnp.sum(block * block))
        half = jnp.dot(
            left_ref[slot], block.astype(jnp.bfloat16), preferred_element_type=jnp.float32
        ).astype(jnp.bfloat16)
        precond = jnp.dot(half, right_ref[slot], preferred_element_type=jnp.float32)
        pre_norm = jnp.sqrt(jnp.sum(precond * precond) + graft_eps)
        grafted = precond * (grad_norm / pre_norm)
        out = jnp.concatenate(
            [
                grafted[:, at : at + LANES].reshape(shards, rows, LANES)
                for at in range(0, order, LANES)
            ],
            axis=1,
        )
        out_ref[:, slot * stacked : (slot + 1) * stacked, :] = out.astype(out_ref.dtype)


def precondition(arrived, left_root, right_root):
    return pl.pallas_call(
        precondition_kernel,
        out_shape=jax.ShapeDtypeStruct(arrived.shape, jnp.bfloat16),
        compiler_params=pltpu.CompilerParams(vmem_limit_bytes=40 * 1024 * 1024),
    )(arrived, left_root, right_root)


def step_kernel(index_ref, returned_ref, momentum_ref, next_ref, *update_refs):
    for part, update_ref in enumerate(update_refs):
        blocks, rows, _ = update_ref.shape

        def one(at, carry):
            block = part * blocks + at
            stacked = returned_ref[index_ref[block]].astype(jnp.float32)
            grafted = jnp.concatenate(
                [stacked[row : row + rows] for row in range(0, stacked.shape[0], rows)], axis=1
            )
            momentum_next = (
                momentum_decay * momentum_ref[block].astype(jnp.float32) + grafted
            ).astype(jnp.bfloat16)
            next_ref[block] = momentum_next
            update_ref[at] = (
                grafted + momentum_decay * momentum_next.astype(jnp.float32)
            ).astype(jnp.bfloat16)
            return carry

        lax.fori_loop(0, blocks, one, 0, unroll=True)


def step(index, returned, momentum):
    blocks, rows, width = momentum.shape
    vmem = pl.BlockSpec(memory_space=pltpu.VMEM)
    half = jax.ShapeDtypeStruct((blocks // 2, rows, width), jnp.bfloat16)
    return pl.pallas_call(
        step_kernel,
        out_shape=(jax.ShapeDtypeStruct(momentum.shape, jnp.bfloat16), half, half),
        in_specs=[pl.BlockSpec(memory_space=pltpu.SMEM), vmem, vmem],
        compiler_params=pltpu.CompilerParams(vmem_limit_bytes=16 * 1024 * 1024),
    )(index, returned, momentum)


def write_kernel(count, places, *refs):
    pieces, out_ref, sems = refs[:count], refs[-2], refs[-1]
    part = lax.axis_index("rep")
    copies = []
    for at, (flip, half) in enumerate(places):
        copies.append(
            pltpu.make_async_copy(pieces[at], out_ref.at[part ^ flip, half], sems.at[at])
        )
        copies[-1].start()
    for copy in copies:
        copy.wait()


def write(pieces, places, shape, held=()):
    anywhere = pl.BlockSpec(memory_space=pl.ANY)
    return pl.pallas_call(
        functools.partial(write_kernel, len(pieces), places),
        out_shape=jax.ShapeDtypeStruct(shape, pieces[0].dtype),
        in_specs=[pl.BlockSpec(memory_space=pltpu.VMEM)] * len(pieces) + [anywhere] * len(held),
        out_specs=anywhere,
        scratch_shapes=[pltpu.SemaphoreType.DMA((len(pieces),))],
        input_output_aliases={len(pieces): 0} if held else {},
        compiler_params=pltpu.CompilerParams(vmem_limit_bytes=8 * 1024 * 1024),
    )(*pieces, *held)


def step_and_gather(index, returned, momentum):
    swap_core = [(at, at ^ 1) for at in range(4)]
    swap_chip = [(at, at ^ 2) for at in range(4)]
    blocks, rows, width = momentum.shape
    half = blocks // 2
    next_rows, *own = step(index, returned, momentum)
    chip = [lax.ppermute(piece, "rep", swap_chip) for piece in own]
    core = [lax.ppermute(piece, "rep", swap_core) for piece in own]
    cross = [lax.ppermute(piece, "rep", swap_core) for piece in chip]
    shape = (4, 2, half, rows, width)
    out = write(own + core, ((0, 0), (0, 1), (1, 0), (1, 1)), shape)
    out = write(chip + cross, ((2, 0), (2, 1), (3, 0), (3, 1)), shape, (out,))
    return next_rows, out.reshape(4 * blocks, rows, width)


def hand_along(owners):
    shards = lax.axis_size("shard")
    for distance in HOPS:
        hops = [
            (part * shards + at, part * shards + (at + distance) % shards)
            for part in range(1, lax.axis_size("rep"), 2)
            for at in range(shards)
        ]
        owners = lax.ppermute(owners, ("rep", "shard"), hops)
    return owners


def local(grad, momentum, owners, left_roots, right_roots):
    shard_count = lax.axis_size("shard")
    capacity = left_roots.shape[2]
    owners = owners.reshape(1, -1)
    outgoing, index = pack(grad, owners, hand_along(owners), shard_count, capacity)
    stacked = outgoing.shape[1]
    outgoing = outgoing.reshape(shard_count, capacity * stacked, LANES)
    arrived = lax.all_to_all(outgoing, "shard", 0, 0, tiled=True)
    grafted = precondition(arrived, left_roots[0, 0], right_roots[0, 0])
    returned = lax.all_to_all(grafted, "shard", 0, 0, tiled=True)
    returned = returned.reshape(shard_count * capacity, stacked, LANES)
    return step_and_gather(index, returned, momentum)


def solution(mesh):
    placed = (
        P("rep", "shard", None),
        P("rep", "shard", None),
        P("rep", None),
        P("rep", "shard", None, None, None),
        P("rep", "shard", None, None, None),
    )
    return jax.shard_map(
        local,
        mesh=mesh,
        in_specs=placed,
        out_specs=(P("rep", "shard", None), P(None, "shard", None)),
        check_vma=False,
    )
```

```python
import functools

import jax
import jax.numpy as jnp
from jax import lax
from jax.experimental import pallas as pl
from jax.experimental.pallas import tpu as pltpu
from jax.sharding import PartitionSpec as P

momentum_decay = 0.9
graft_eps = 1e-06
LANES = 128
HOPS = (36, 2)


def pack_kernel(owner_ref, grad_ref, out_ref, index_ref, count_ref):
    owners, capacity = count_ref.shape[0], out_ref.shape[0] // count_ref.shape[0]
    blocks, _, width = grad_ref.shape
    out_ref[...] = jnp.zeros_like(out_ref)

    def clear(at, carry):
        count_ref[at] = 0
        return carry

    lax.fori_loop(0, owners, clear, 0, unroll=True)

    def place(block, carry):
        owner = owner_ref[0, block]
        slot = count_ref[owner]
        count_ref[owner] = slot + 1
        index = owner * capacity + slot
        index_ref[block] = index
        rows = grad_ref[block]
        stacked = jnp.concatenate(
            [rows[:, at : at + LANES] for at in range(0, width, LANES)], axis=0
        )
        out_ref[index] = stacked.astype(out_ref.dtype)
        return carry

    lax.fori_loop(0, blocks, place, 0, unroll=True)


def pack(grad, owners, shard_count, capacity):
    blocks, rows, width = grad.shape
    stacked_rows = rows * (width // LANES)
    return pl.pallas_call(
        pack_kernel,
        out_shape=(
            jax.ShapeDtypeStruct((shard_count * capacity, stacked_rows, LANES), jnp.bfloat16),
            jax.ShapeDtypeStruct((blocks,), jnp.int32),
        ),
        in_specs=[
            pl.BlockSpec(memory_space=pltpu.SMEM),
            pl.BlockSpec(memory_space=pltpu.VMEM),
        ],
        out_specs=(
            pl.BlockSpec(memory_space=pltpu.VMEM),
            pl.BlockSpec(memory_space=pltpu.SMEM),
        ),
        scratch_shapes=[pltpu.SMEM((shard_count,), jnp.int32)],
        compiler_params=pltpu.CompilerParams(vmem_limit_bytes=16 * 1024 * 1024),
    )(owners, grad)


def precondition_kernel(arrived_ref, left_ref, right_ref, out_ref):
    shards, slot_rows, _ = arrived_ref.shape
    capacity, order, _ = left_ref.shape
    stacked = slot_rows // capacity
    rows = order // shards
    slots = range(capacity)
    blocks = []
    for slot in slots:
        pieces = arrived_ref[:, slot * stacked : (slot + 1) * stacked, :].astype(jnp.float32)
        blocks.append(
            jnp.concatenate(
                [
                    pieces[:, at : at + rows, :].reshape(order, LANES)
                    for at in range(0, stacked, rows)
                ],
                axis=1,
            )
        )
    halves = [
        jnp.dot(
            left_ref[slot], blocks[slot].astype(jnp.bfloat16), preferred_element_type=jnp.float32
        ).astype(jnp.bfloat16)
        for slot in slots
    ]
    preconds = [
        jnp.dot(halves[slot], right_ref[slot], preferred_element_type=jnp.float32)
        for slot in slots
    ]
    for slot in slots:
        grad_square = jnp.sum(blocks[slot] * blocks[slot])
        pre_square = jnp.sum(preconds[slot] * preconds[slot]) + graft_eps
        grafted = preconds[slot] * (jnp.sqrt(grad_square) / jnp.sqrt(pre_square))
        out = jnp.concatenate(
            [
                grafted[:, at : at + LANES].reshape(shards, rows, LANES)
                for at in range(0, order, LANES)
            ],
            axis=1,
        )
        out_ref[:, slot * stacked : (slot + 1) * stacked, :] = out.astype(out_ref.dtype)


def precondition(arrived, left_root, right_root):
    return pl.pallas_call(
        precondition_kernel,
        out_shape=jax.ShapeDtypeStruct(arrived.shape, jnp.bfloat16),
        compiler_params=pltpu.CompilerParams(vmem_limit_bytes=40 * 1024 * 1024),
    )(arrived, left_root, right_root)


def step_kernel(index_ref, returned_ref, momentum_ref, next_ref, *update_refs):
    for part, update_ref in enumerate(update_refs):
        blocks, rows, _ = update_ref.shape

        def one(at, carry):
            block = part * blocks + at
            stacked = returned_ref[index_ref[block]].astype(jnp.float32)
            grafted = jnp.concatenate(
                [stacked[row : row + rows] for row in range(0, stacked.shape[0], rows)], axis=1
            )
            momentum_next = (
                momentum_decay * momentum_ref[block].astype(jnp.float32) + grafted
            ).astype(jnp.bfloat16)
            next_ref[block] = momentum_next
            update_ref[at] = (
                grafted + momentum_decay * momentum_next.astype(jnp.float32)
            ).astype(jnp.bfloat16)
            return carry

        lax.fori_loop(0, blocks, one, 0, unroll=True)


def step(index, returned, momentum):
    blocks, rows, width = momentum.shape
    vmem = pl.BlockSpec(memory_space=pltpu.VMEM)
    half = jax.ShapeDtypeStruct((blocks // 2, rows, width), jnp.bfloat16)
    return pl.pallas_call(
        step_kernel,
        out_shape=(jax.ShapeDtypeStruct(momentum.shape, jnp.bfloat16), half, half),
        in_specs=[pl.BlockSpec(memory_space=pltpu.SMEM), vmem, vmem],
        compiler_params=pltpu.CompilerParams(vmem_limit_bytes=16 * 1024 * 1024),
    )(index, returned, momentum)


def write_kernel(count, places, *refs):
    pieces, out_ref, sems = refs[:count], refs[-2], refs[-1]
    part = lax.axis_index("rep")
    copies = []
    for at, (flip, half) in enumerate(places):
        copies.append(
            pltpu.make_async_copy(pieces[at], out_ref.at[part ^ flip, half], sems.at[at])
        )
        copies[-1].start()
    for copy in copies:
        copy.wait()


def write(pieces, places, shape, held=()):
    anywhere = pl.BlockSpec(memory_space=pl.ANY)
    return pl.pallas_call(
        functools.partial(write_kernel, len(pieces), places),
        out_shape=jax.ShapeDtypeStruct(shape, pieces[0].dtype),
        in_specs=[pl.BlockSpec(memory_space=pltpu.VMEM)] * len(pieces) + [anywhere] * len(held),
        out_specs=anywhere,
        scratch_shapes=[pltpu.SemaphoreType.DMA((len(pieces),))],
        input_output_aliases={len(pieces): 0} if held else {},
        compiler_params=pltpu.CompilerParams(vmem_limit_bytes=8 * 1024 * 1024),
    )(*pieces, *held)


def gather_parts(own, blocks):
    swap_core = [(at, at ^ 1) for at in range(4)]
    swap_chip = [(at, at ^ 2) for at in range(4)]
    half, rows, width = own[0].shape
    chip = [lax.ppermute(piece, "rep", swap_chip) for piece in own]
    core = [lax.ppermute(piece, "rep", swap_core) for piece in own]
    cross = [lax.ppermute(piece, "rep", swap_core) for piece in chip]
    shape = (4, 2, half, rows, width)
    out = write(own + core, ((0, 0), (0, 1), (1, 0), (1, 1)), shape)
    out = write(chip + cross, ((2, 0), (2, 1), (3, 0), (3, 1)), shape, (out,))
    return out.reshape(4 * blocks, rows, width)


def swap_rows(rows):
    return lax.all_to_all(rows, "shard", 0, 0, tiled=True)


def early(grad, momentum, owners, left_root, right_root):
    shards, capacity = lax.axis_size("shard"), left_root.shape[0]
    outgoing, index = pack(grad, owners, shards, capacity)
    stacked = outgoing.shape[1]
    arrived = swap_rows(outgoing.reshape(shards, capacity * stacked, LANES))
    returned = swap_rows(precondition(arrived, left_root, right_root))
    return step(index, returned.reshape(shards * capacity, stacked, LANES), momentum)


def late(grad, momentum, owners, left_root, right_root):
    shards = lax.axis_size("shard")
    for distance in HOPS:
        hops = [
            (part * shards + at, part * shards + (at + distance) % shards)
            for part in range(1, lax.axis_size("rep"), 2)
            for at in range(shards)
        ]
        owners = lax.ppermute(owners, ("rep", "shard"), hops)
    return early(grad, momentum, owners, left_root, right_root)


def local(grad, momentum, owners, left_roots, right_roots):
    odd = lax.rem(lax.axis_index("rep"), 2) == 1
    next_rows, *own = lax.cond(
        odd,
        late,
        early,
        grad,
        momentum,
        owners.reshape(1, -1),
        left_roots[0, 0],
        right_roots[0, 0],
    )
    return next_rows, gather_parts(own, momentum.shape[0])


def solution(mesh):
    placed = (
        P("rep", "shard", None),
        P("rep", "shard", None),
        P("rep", None),
        P("rep", "shard", None, None, None),
        P("rep", "shard", None, None, None),
    )
    return jax.shard_map(
        local,
        mesh=mesh,
        in_specs=placed,
        out_specs=(P("rep", "shard", None), P(None, "shard", None)),
        check_vma=False,
    )
```

```python
import functools

import jax
import jax.numpy as jnp
from jax import lax
from jax.experimental import pallas as pl
from jax.experimental.pallas import tpu as pltpu
from jax.sharding import PartitionSpec as P

momentum_decay = 0.9
graft_eps = 1e-06
LANES = 128
HOPS = (36, 2)
PIECES = (16, 16)


def pack_kernel(owner_ref, grad_ref, out_ref, index_ref, count_ref):
    owners, capacity = count_ref.shape[0], out_ref.shape[0] // count_ref.shape[0]
    blocks, _, width = grad_ref.shape
    out_ref[...] = jnp.zeros_like(out_ref)

    def clear(at, carry):
        count_ref[at] = 0
        return carry

    lax.fori_loop(0, owners, clear, 0, unroll=True)

    def place(block, carry):
        owner = owner_ref[0, block]
        slot = count_ref[owner]
        count_ref[owner] = slot + 1
        index = owner * capacity + slot
        index_ref[block] = index
        rows = grad_ref[block]
        stacked = jnp.concatenate(
            [rows[:, at : at + LANES] for at in range(0, width, LANES)], axis=0
        )
        out_ref[index] = stacked.astype(out_ref.dtype)
        return carry

    lax.fori_loop(0, blocks, place, 0, unroll=True)


def pack(grad, owners, shard_count, capacity):
    blocks, rows, width = grad.shape
    stacked_rows = rows * (width // LANES)
    return pl.pallas_call(
        pack_kernel,
        out_shape=(
            jax.ShapeDtypeStruct((shard_count * capacity, stacked_rows, LANES), jnp.bfloat16),
            jax.ShapeDtypeStruct((blocks,), jnp.int32),
        ),
        in_specs=[
            pl.BlockSpec(memory_space=pltpu.SMEM),
            pl.BlockSpec(memory_space=pltpu.VMEM),
        ],
        out_specs=(
            pl.BlockSpec(memory_space=pltpu.VMEM),
            pl.BlockSpec(memory_space=pltpu.SMEM),
        ),
        scratch_shapes=[pltpu.SMEM((shard_count,), jnp.int32)],
        compiler_params=pltpu.CompilerParams(vmem_limit_bytes=16 * 1024 * 1024),
    )(owners, grad)


def precondition_kernel(arrived_ref, left_ref, right_ref, out_ref):
    shards, slot_rows, _ = arrived_ref.shape
    capacity, order, _ = left_ref.shape
    stacked = slot_rows // capacity
    rows = order // shards
    slots = range(capacity)
    blocks = []
    for slot in slots:
        pieces = arrived_ref[:, slot * stacked : (slot + 1) * stacked, :].astype(jnp.float32)
        blocks.append(
            jnp.concatenate(
                [
                    pieces[:, at : at + rows, :].reshape(order, LANES)
                    for at in range(0, stacked, rows)
                ],
                axis=1,
            )
        )
    halves = [
        jnp.dot(
            left_ref[slot], blocks[slot].astype(jnp.bfloat16), preferred_element_type=jnp.float32
        ).astype(jnp.bfloat16)
        for slot in slots
    ]
    preconds = [
        jnp.dot(halves[slot], right_ref[slot], preferred_element_type=jnp.float32)
        for slot in slots
    ]
    for slot in slots:
        grad_square = jnp.sum(blocks[slot] * blocks[slot])
        pre_square = jnp.sum(preconds[slot] * preconds[slot]) + graft_eps
        grafted = preconds[slot] * (jnp.sqrt(grad_square) / jnp.sqrt(pre_square))
        out = jnp.concatenate(
            [
                grafted[:, at : at + LANES].reshape(shards, rows, LANES)
                for at in range(0, order, LANES)
            ],
            axis=1,
        )
        out_ref[:, slot * stacked : (slot + 1) * stacked, :] = out.astype(out_ref.dtype)


def precondition(arrived, left_root, right_root):
    return pl.pallas_call(
        precondition_kernel,
        out_shape=jax.ShapeDtypeStruct(arrived.shape, jnp.bfloat16),
        compiler_params=pltpu.CompilerParams(vmem_limit_bytes=40 * 1024 * 1024),
    )(arrived, left_root, right_root)


def step_kernel(index_ref, returned_ref, momentum_ref, next_ref, *update_refs):
    first = 0
    for update_ref in update_refs:
        blocks, rows, _ = update_ref.shape

        def one(at, carry):
            block = first + at
            stacked = returned_ref[index_ref[block]].astype(jnp.float32)
            grafted = jnp.concatenate(
                [stacked[row : row + rows] for row in range(0, stacked.shape[0], rows)], axis=1
            )
            momentum_next = (
                momentum_decay * momentum_ref[block].astype(jnp.float32) + grafted
            ).astype(jnp.bfloat16)
            next_ref[block] = momentum_next
            update_ref[at] = (
                grafted + momentum_decay * momentum_next.astype(jnp.float32)
            ).astype(jnp.bfloat16)
            return carry

        lax.fori_loop(0, blocks, one, 0, unroll=True)
        first += blocks


def step(index, returned, momentum):
    _, rows, width = momentum.shape
    vmem = pl.BlockSpec(memory_space=pltpu.VMEM)
    pieces = [jax.ShapeDtypeStruct((count, rows, width), jnp.bfloat16) for count in PIECES]
    return pl.pallas_call(
        step_kernel,
        out_shape=(jax.ShapeDtypeStruct(momentum.shape, jnp.bfloat16), *pieces),
        in_specs=[pl.BlockSpec(memory_space=pltpu.SMEM), vmem, vmem],
        compiler_params=pltpu.CompilerParams(vmem_limit_bytes=16 * 1024 * 1024),
    )(index, returned, momentum)


def write_kernel(places, *refs):
    count = len(places)
    pieces, sems = refs[:count], refs[-1]
    part = lax.axis_index("rep")
    whole = len(refs) == count + 4
    out_ref = refs[-3] if whole else refs[-2]
    copies = []
    for at, (flip, first) in enumerate(places):
        run = pl.ds(first, pieces[at].shape[0])
        copies.append(
            pltpu.make_async_copy(pieces[at], out_ref.at[part ^ flip, run], sems.at[at])
        )
    if whole:
        copies.append(pltpu.make_async_copy(refs[count], refs[-2], sems.at[count]))
    for copy in copies:
        copy.start()
    for copy in copies:
        copy.wait()


def write(pieces, places, shape, held=None, whole=None):
    anywhere = pl.BlockSpec(memory_space=pl.ANY)
    vmem = pl.BlockSpec(memory_space=pltpu.VMEM)
    operands, in_specs = list(pieces), [vmem] * len(pieces)
    out_shape, aliases = [jax.ShapeDtypeStruct(shape, pieces[0].dtype)], {}
    if whole is not None:
        operands, in_specs = operands + [whole], in_specs + [vmem]
        out_shape.append(jax.ShapeDtypeStruct(whole.shape, whole.dtype))
    if held is not None:
        aliases = {len(operands): 0}
        operands, in_specs = operands + [held], in_specs + [anywhere]
    return pl.pallas_call(
        functools.partial(write_kernel, places),
        out_shape=out_shape,
        in_specs=in_specs,
        out_specs=[anywhere] * len(out_shape),
        scratch_shapes=[pltpu.SemaphoreType.DMA((len(pieces) + 1,))],
        input_output_aliases=aliases,
        compiler_params=pltpu.CompilerParams(vmem_limit_bytes=8 * 1024 * 1024),
    )(*operands)


def gather_parts(next_rows, own):
    swap_core = [(at, at ^ 1) for at in range(4)]
    swap_chip = [(at, at ^ 2) for at in range(4)]
    chip = [lax.ppermute(piece, "rep", swap_chip) for piece in own]
    core = [lax.ppermute(piece, "rep", swap_core) for piece in own]
    cross = [lax.ppermute(piece, "rep", swap_core) for piece in chip]
    blocks, rows, width = next_rows.shape
    shape = (4, blocks, rows, width)
    at = (0, PIECES[0])
    places = [tuple((flip, first) for flip in flips for first in at) for flips in ((0, 1), (2, 3))]
    out, next_rows = write(own + core, places[0], shape, whole=next_rows)
    (out,) = write(chip + cross, places[1], shape, held=out)
    return next_rows, out.reshape(4 * blocks, rows, width)


def swap_rows(rows):
    return lax.all_to_all(rows, "shard", 0, 0, tiled=True)


def early(grad, momentum, owners, left_root, right_root):
    shards, capacity = lax.axis_size("shard"), left_root.shape[0]
    outgoing, index = pack(grad, owners, shards, capacity)
    stacked = outgoing.shape[1]
    arrived = swap_rows(outgoing.reshape(shards, capacity * stacked, LANES))
    returned = swap_rows(precondition(arrived, left_root, right_root))
    return step(index, returned.reshape(shards * capacity, stacked, LANES), momentum)


def late(grad, momentum, owners, left_root, right_root):
    shards = lax.axis_size("shard")
    for distance in HOPS:
        hops = [
            (part * shards + at, part * shards + (at + distance) % shards)
            for part in range(1, lax.axis_size("rep"), 2)
            for at in range(shards)
        ]
        owners = lax.ppermute(owners, ("rep", "shard"), hops)
    return early(grad, momentum, owners, left_root, right_root)


def local(grad, momentum, owners, left_roots, right_roots):
    odd = lax.rem(lax.axis_index("rep"), 2) == 1
    next_rows, *own = lax.cond(
        odd,
        late,
        early,
        grad,
        momentum,
        owners.reshape(1, -1),
        left_roots[0, 0],
        right_roots[0, 0],
    )
    return gather_parts(next_rows, own)


def solution(mesh):
    placed = (
        P("rep", "shard", None),
        P("rep", "shard", None),
        P("rep", None),
        P("rep", "shard", None, None, None),
        P("rep", "shard", None, None, None),
    )
    return jax.shard_map(
        local,
        mesh=mesh,
        in_specs=placed,
        out_specs=(P("rep", "shard", None), P(None, "shard", None)),
        check_vma=False,
    )
```

```python
import functools

import jax
import jax.numpy as jnp
from jax import lax
from jax.experimental import pallas as pl
from jax.experimental.pallas import tpu as pltpu
from jax.sharding import PartitionSpec as P

momentum_decay = 0.9
graft_eps = 1e-06
LANES = 128
HOPS = (36, 2)
PIECES = (16, 16)


def pack_kernel(owner_ref, grad_ref, out_ref, index_ref, count_ref):
    owners, capacity = count_ref.shape[0], out_ref.shape[0] // count_ref.shape[0]
    blocks, _, width = grad_ref.shape
    out_ref[...] = jnp.zeros_like(out_ref)

    def clear(at, carry):
        count_ref[at] = 0
        return carry

    lax.fori_loop(0, owners, clear, 0, unroll=True)

    def place(block, carry):
        owner = owner_ref[0, block]
        slot = count_ref[owner]
        count_ref[owner] = slot + 1
        index = owner * capacity + slot
        index_ref[block] = index
        rows = grad_ref[block]
        stacked = jnp.concatenate(
            [rows[:, at : at + LANES] for at in range(0, width, LANES)], axis=0
        )
        out_ref[index] = stacked.astype(out_ref.dtype)
        return carry

    lax.fori_loop(0, blocks, place, 0, unroll=True)


def pack(grad, owners, shard_count, capacity):
    blocks, rows, width = grad.shape
    stacked_rows = rows * (width // LANES)
    return pl.pallas_call(
        pack_kernel,
        out_shape=(
            jax.ShapeDtypeStruct((shard_count * capacity, stacked_rows, LANES), jnp.bfloat16),
            jax.ShapeDtypeStruct((blocks,), jnp.int32),
        ),
        in_specs=[
            pl.BlockSpec(memory_space=pltpu.SMEM),
            pl.BlockSpec(memory_space=pltpu.VMEM),
        ],
        out_specs=(
            pl.BlockSpec(memory_space=pltpu.VMEM),
            pl.BlockSpec(memory_space=pltpu.SMEM),
        ),
        scratch_shapes=[pltpu.SMEM((shard_count,), jnp.int32)],
        compiler_params=pltpu.CompilerParams(vmem_limit_bytes=16 * 1024 * 1024),
    )(owners, grad)


def precondition_kernel(arrived_ref, left_ref, right_ref, out_ref):
    shards, slot_rows, _ = arrived_ref.shape
    capacity, order, _ = left_ref.shape
    stacked = slot_rows // capacity
    rows = order // shards
    slots = range(capacity)
    blocks = []
    for slot in slots:
        pieces = arrived_ref[:, slot * stacked : (slot + 1) * stacked, :].astype(jnp.float32)
        blocks.append(
            jnp.concatenate(
                [
                    pieces[:, at : at + rows, :].reshape(order, LANES)
                    for at in range(0, stacked, rows)
                ],
                axis=1,
            )
        )
    halves = [
        jnp.dot(
            left_ref[slot], blocks[slot].astype(jnp.bfloat16), preferred_element_type=jnp.float32
        ).astype(jnp.bfloat16)
        for slot in slots
    ]
    preconds = [
        jnp.dot(halves[slot], right_ref[slot], preferred_element_type=jnp.float32)
        for slot in slots
    ]
    for slot in slots:
        grad_square = jnp.sum(blocks[slot] * blocks[slot])
        pre_square = jnp.sum(preconds[slot] * preconds[slot]) + graft_eps
        grafted = preconds[slot] * (jnp.sqrt(grad_square) / jnp.sqrt(pre_square))
        out = jnp.concatenate(
            [
                grafted[:, at : at + LANES].reshape(shards, rows, LANES)
                for at in range(0, order, LANES)
            ],
            axis=1,
        )
        out_ref[:, slot * stacked : (slot + 1) * stacked, :] = out.astype(out_ref.dtype)


def precondition(arrived, left_root, right_root):
    return pl.pallas_call(
        precondition_kernel,
        out_shape=jax.ShapeDtypeStruct(arrived.shape, jnp.bfloat16),
        compiler_params=pltpu.CompilerParams(vmem_limit_bytes=40 * 1024 * 1024),
    )(arrived, left_root, right_root)


def step_kernel(index_ref, returned_ref, momentum_ref, next_ref, *update_refs):
    first = 0
    for update_ref in update_refs:
        blocks, rows, _ = update_ref.shape

        def one(at, carry):
            block = first + at
            stacked = returned_ref[index_ref[block]].astype(jnp.float32)
            grafted = jnp.concatenate(
                [stacked[row : row + rows] for row in range(0, stacked.shape[0], rows)], axis=1
            )
            momentum_next = (
                momentum_decay * momentum_ref[block].astype(jnp.float32) + grafted
            ).astype(jnp.bfloat16)
            next_ref[block] = momentum_next
            update_ref[at] = (
                grafted + momentum_decay * momentum_next.astype(jnp.float32)
            ).astype(jnp.bfloat16)
            return carry

        lax.fori_loop(0, blocks, one, 0, unroll=True)
        first += blocks


def step(index, returned, momentum):
    _, rows, width = momentum.shape
    vmem = pl.BlockSpec(memory_space=pltpu.VMEM)
    pieces = [jax.ShapeDtypeStruct((count, rows, width), jnp.bfloat16) for count in PIECES]
    return pl.pallas_call(
        step_kernel,
        out_shape=(jax.ShapeDtypeStruct(momentum.shape, jnp.bfloat16), *pieces),
        in_specs=[pl.BlockSpec(memory_space=pltpu.SMEM), vmem, vmem],
        compiler_params=pltpu.CompilerParams(vmem_limit_bytes=16 * 1024 * 1024),
    )(index, returned, momentum)


def write_kernel(places, *refs):
    count = len(places)
    pieces, sems = refs[:count], refs[-1]
    part = lax.axis_index("rep")
    whole = len(refs) == count + 4
    out_ref = refs[-3] if whole else refs[-2]
    copies = []
    for at, (flip, first) in enumerate(places):
        run = pl.ds(first, pieces[at].shape[0])
        copies.append(
            pltpu.make_async_copy(pieces[at], out_ref.at[part ^ flip, run], sems.at[at])
        )
    if whole:
        copies.append(pltpu.make_async_copy(refs[count], refs[-2], sems.at[count]))
    for copy in copies:
        copy.start()
    for copy in copies:
        copy.wait()


def write(pieces, places, shape, held=None, whole=None):
    anywhere = pl.BlockSpec(memory_space=pl.ANY)
    vmem = pl.BlockSpec(memory_space=pltpu.VMEM)
    operands, in_specs = list(pieces), [vmem] * len(pieces)
    out_shape, aliases = [jax.ShapeDtypeStruct(shape, pieces[0].dtype)], {}
    if whole is not None:
        operands, in_specs = operands + [whole], in_specs + [vmem]
        out_shape.append(jax.ShapeDtypeStruct(whole.shape, whole.dtype))
    if held is not None:
        aliases = {len(operands): 0}
        operands, in_specs = operands + [held], in_specs + [anywhere]
    return pl.pallas_call(
        functools.partial(write_kernel, places),
        out_shape=out_shape,
        in_specs=in_specs,
        out_specs=[anywhere] * len(out_shape),
        scratch_shapes=[pltpu.SemaphoreType.DMA((len(pieces) + 1,))],
        input_output_aliases=aliases,
        compiler_params=pltpu.CompilerParams(vmem_limit_bytes=8 * 1024 * 1024),
    )(*operands)


def gather_parts(next_rows, own):
    swap_core = [(at, at ^ 1) for at in range(4)]
    swap_chip = [(at, at ^ 2) for at in range(4)]
    chip = [lax.ppermute(piece, "rep", swap_chip) for piece in own]
    core = [lax.ppermute(piece, "rep", swap_core) for piece in own]
    cross = [lax.ppermute(piece, "rep", swap_core) for piece in chip]
    blocks, rows, width = next_rows.shape
    shape = (4, blocks, rows, width)
    starts = [sum(PIECES[:at]) for at in range(len(PIECES))]
    last = starts[-1]
    places = [(flip, first) for flip in (0, 1, 2) for first in starts]
    places += [(3, first) for first in starts[:-1]]
    pieces = own + core + chip + cross[:-1]
    out, next_rows = write(pieces, tuple(places), shape, whole=next_rows)
    (out,) = write(cross[-1:], ((3, last),), shape, held=out)
    return next_rows, out.reshape(4 * blocks, rows, width)


def swap_rows(rows):
    return lax.all_to_all(rows, "shard", 0, 0, tiled=True)


def early(grad, momentum, owners, left_root, right_root):
    shards, capacity = lax.axis_size("shard"), left_root.shape[0]
    outgoing, index = pack(grad, owners, shards, capacity)
    stacked = outgoing.shape[1]
    arrived = swap_rows(outgoing.reshape(shards, capacity * stacked, LANES))
    returned = swap_rows(precondition(arrived, left_root, right_root))
    return step(index, returned.reshape(shards * capacity, stacked, LANES), momentum)


def late(grad, momentum, owners, left_root, right_root):
    shards = lax.axis_size("shard")
    for distance in HOPS:
        hops = [
            (part * shards + at, part * shards + (at + distance) % shards)
            for part in range(1, lax.axis_size("rep"), 2)
            for at in range(shards)
        ]
        owners = lax.ppermute(owners, ("rep", "shard"), hops)
    return early(grad, momentum, owners, left_root, right_root)


def local(grad, momentum, owners, left_roots, right_roots):
    odd = lax.rem(lax.axis_index("rep"), 2) == 1
    next_rows, *own = lax.cond(
        odd,
        late,
        early,
        grad,
        momentum,
        owners.reshape(1, -1),
        left_roots[0, 0],
        right_roots[0, 0],
    )
    return gather_parts(next_rows, own)


def solution(mesh):
    placed = (
        P("rep", "shard", None),
        P("rep", "shard", None),
        P("rep", None),
        P("rep", "shard", None, None, None),
        P("rep", "shard", None, None, None),
    )
    return jax.shard_map(
        local,
        mesh=mesh,
        in_specs=placed,
        out_specs=(P("rep", "shard", None), P(None, "shard", None)),
        check_vma=False,
    )
```

```python
import functools

import jax
import jax.numpy as jnp
from jax import lax
from jax.experimental import pallas as pl
from jax.experimental.pallas import tpu as pltpu
from jax.sharding import PartitionSpec as P

momentum_decay = 0.9
graft_eps = 1e-06
LANES = 128
HOPS = (20, 2)
PIECES = (20, 12)


def pack_kernel(owner_ref, grad_ref, out_ref, index_ref, count_ref):
    owners, capacity = count_ref.shape[0], out_ref.shape[0] // count_ref.shape[0]
    blocks, _, width = grad_ref.shape
    out_ref[...] = jnp.zeros_like(out_ref)

    def clear(at, carry):
        count_ref[at] = 0
        return carry

    lax.fori_loop(0, owners, clear, 0, unroll=True)

    def place(block, carry):
        owner = owner_ref[0, block]
        slot = count_ref[owner]
        count_ref[owner] = slot + 1
        index = owner * capacity + slot
        index_ref[block] = index
        rows = grad_ref[block]
        stacked = jnp.concatenate(
            [rows[:, at : at + LANES] for at in range(0, width, LANES)], axis=0
        )
        out_ref[index] = stacked.astype(out_ref.dtype)
        return carry

    lax.fori_loop(0, blocks, place, 0, unroll=True)


def pack(grad, owners, shard_count, capacity):
    blocks, rows, width = grad.shape
    stacked_rows = rows * (width // LANES)
    return pl.pallas_call(
        pack_kernel,
        out_shape=(
            jax.ShapeDtypeStruct((shard_count * capacity, stacked_rows, LANES), jnp.bfloat16),
            jax.ShapeDtypeStruct((blocks,), jnp.int32),
        ),
        in_specs=[
            pl.BlockSpec(memory_space=pltpu.SMEM),
            pl.BlockSpec(memory_space=pltpu.VMEM),
        ],
        out_specs=(
            pl.BlockSpec(memory_space=pltpu.VMEM),
            pl.BlockSpec(memory_space=pltpu.SMEM),
        ),
        scratch_shapes=[pltpu.SMEM((shard_count,), jnp.int32)],
        compiler_params=pltpu.CompilerParams(vmem_limit_bytes=16 * 1024 * 1024),
    )(owners, grad)


def precondition_kernel(arrived_ref, left_ref, right_ref, out_ref):
    shards, slot_rows, _ = arrived_ref.shape
    capacity, order, _ = left_ref.shape
    stacked = slot_rows // capacity
    rows = order // shards
    slots = range(capacity)
    blocks = []
    for slot in slots:
        pieces = arrived_ref[:, slot * stacked : (slot + 1) * stacked, :].astype(jnp.float32)
        blocks.append(
            jnp.concatenate(
                [
                    pieces[:, at : at + rows, :].reshape(order, LANES)
                    for at in range(0, stacked, rows)
                ],
                axis=1,
            )
        )
    halves = [
        jnp.dot(
            left_ref[slot], blocks[slot].astype(jnp.bfloat16), preferred_element_type=jnp.float32
        ).astype(jnp.bfloat16)
        for slot in slots
    ]
    preconds = [
        jnp.dot(halves[slot], right_ref[slot], preferred_element_type=jnp.float32)
        for slot in slots
    ]
    for slot in slots:
        grad_square = jnp.sum(blocks[slot] * blocks[slot])
        pre_square = jnp.sum(preconds[slot] * preconds[slot]) + graft_eps
        grafted = preconds[slot] * (jnp.sqrt(grad_square) / jnp.sqrt(pre_square))
        out = jnp.concatenate(
            [
                grafted[:, at : at + LANES].reshape(shards, rows, LANES)
                for at in range(0, order, LANES)
            ],
            axis=1,
        )
        out_ref[:, slot * stacked : (slot + 1) * stacked, :] = out.astype(out_ref.dtype)


def precondition(arrived, left_root, right_root):
    return pl.pallas_call(
        precondition_kernel,
        out_shape=jax.ShapeDtypeStruct(arrived.shape, jnp.bfloat16),
        compiler_params=pltpu.CompilerParams(vmem_limit_bytes=40 * 1024 * 1024),
    )(arrived, left_root, right_root)


def step_kernel(index_ref, returned_ref, momentum_ref, next_ref, *update_refs):
    first = 0
    for update_ref in update_refs:
        blocks, rows, _ = update_ref.shape

        def one(at, carry):
            block = first + at
            stacked = returned_ref[index_ref[block]].astype(jnp.float32)
            grafted = jnp.concatenate(
                [stacked[row : row + rows] for row in range(0, stacked.shape[0], rows)], axis=1
            )
            momentum_next = (
                momentum_decay * momentum_ref[block].astype(jnp.float32) + grafted
            ).astype(jnp.bfloat16)
            next_ref[block] = momentum_next
            update_ref[at] = (
                grafted + momentum_decay * momentum_next.astype(jnp.float32)
            ).astype(jnp.bfloat16)
            return carry

        lax.fori_loop(0, blocks, one, 0, unroll=True)
        first += blocks


def step(index, returned, momentum):
    _, rows, width = momentum.shape
    vmem = pl.BlockSpec(memory_space=pltpu.VMEM)
    pieces = [jax.ShapeDtypeStruct((count, rows, width), jnp.bfloat16) for count in PIECES]
    return pl.pallas_call(
        step_kernel,
        out_shape=(jax.ShapeDtypeStruct(momentum.shape, jnp.bfloat16), *pieces),
        in_specs=[pl.BlockSpec(memory_space=pltpu.SMEM), vmem, vmem],
        compiler_params=pltpu.CompilerParams(vmem_limit_bytes=16 * 1024 * 1024),
    )(index, returned, momentum)


def write_kernel(places, *refs):
    count = len(places)
    pieces, sems = refs[:count], refs[-1]
    part = lax.axis_index("rep")
    whole = len(refs) == count + 4
    out_ref = refs[-3] if whole else refs[-2]
    copies = []
    for at, (flip, first) in enumerate(places):
        run = pl.ds(first, pieces[at].shape[0])
        copies.append(
            pltpu.make_async_copy(pieces[at], out_ref.at[part ^ flip, run], sems.at[at])
        )
    if whole:
        copies.append(pltpu.make_async_copy(refs[count], refs[-2], sems.at[count]))
    for copy in copies:
        copy.start()
    for copy in copies:
        copy.wait()


def write(pieces, places, shape, held=None, whole=None):
    anywhere = pl.BlockSpec(memory_space=pl.ANY)
    vmem = pl.BlockSpec(memory_space=pltpu.VMEM)
    operands, in_specs = list(pieces), [vmem] * len(pieces)
    out_shape, aliases = [jax.ShapeDtypeStruct(shape, pieces[0].dtype)], {}
    if whole is not None:
        operands, in_specs = operands + [whole], in_specs + [vmem]
        out_shape.append(jax.ShapeDtypeStruct(whole.shape, whole.dtype))
    if held is not None:
        aliases = {len(operands): 0}
        operands, in_specs = operands + [held], in_specs + [anywhere]
    return pl.pallas_call(
        functools.partial(write_kernel, places),
        out_shape=out_shape,
        in_specs=in_specs,
        out_specs=[anywhere] * len(out_shape),
        scratch_shapes=[pltpu.SemaphoreType.DMA((len(pieces) + 1,))],
        input_output_aliases=aliases,
        compiler_params=pltpu.CompilerParams(vmem_limit_bytes=8 * 1024 * 1024),
    )(*operands)


def gather_parts(next_rows, own):
    swap_core = [(at, at ^ 1) for at in range(4)]
    swap_chip = [(at, at ^ 2) for at in range(4)]
    chip = [lax.ppermute(piece, "rep", swap_chip) for piece in own]
    core = [lax.ppermute(piece, "rep", swap_core) for piece in own]
    cross = [lax.ppermute(piece, "rep", swap_core) for piece in chip]
    blocks, rows, width = next_rows.shape
    shape = (4, blocks, rows, width)
    starts = [sum(PIECES[:at]) for at in range(len(PIECES))]
    last = starts[-1]
    places = [(flip, first) for flip in (0, 1, 2) for first in starts]
    places += [(3, first) for first in starts[:-1]]
    pieces = own + core + chip + cross[:-1]
    out, next_rows = write(pieces, tuple(places), shape, whole=next_rows)
    (out,) = write(cross[-1:], ((3, last),), shape, held=out)
    return next_rows, out.reshape(4 * blocks, rows, width)


def swap_rows(rows):
    return lax.all_to_all(rows, "shard", 0, 0, tiled=True)


def early(grad, momentum, owners, left_root, right_root):
    shards, capacity = lax.axis_size("shard"), left_root.shape[0]
    outgoing, index = pack(grad, owners, shards, capacity)
    stacked = outgoing.shape[1]
    arrived = swap_rows(outgoing.reshape(shards, capacity * stacked, LANES))
    returned = swap_rows(precondition(arrived, left_root, right_root))
    return step(index, returned.reshape(shards * capacity, stacked, LANES), momentum)


def late(grad, momentum, owners, left_root, right_root):
    shards = lax.axis_size("shard")
    for distance in HOPS:
        hops = [
            (part * shards + at, part * shards + (at + distance) % shards)
            for part in range(1, lax.axis_size("rep"), 2)
            for at in range(shards)
        ]
        owners = lax.ppermute(owners, ("rep", "shard"), hops)
    return early(grad, momentum, owners, left_root, right_root)


def local(grad, momentum, owners, left_roots, right_roots):
    odd = lax.rem(lax.axis_index("rep"), 2) == 1
    next_rows, *own = lax.cond(
        odd,
        late,
        early,
        grad,
        momentum,
        owners.reshape(1, -1),
        left_roots[0, 0],
        right_roots[0, 0],
    )
    return gather_parts(next_rows, own)


def solution(mesh):
    placed = (
        P("rep", "shard", None),
        P("rep", "shard", None),
        P("rep", None),
        P("rep", "shard", None, None, None),
        P("rep", "shard", None, None, None),
    )
    return jax.shard_map(
        local,
        mesh=mesh,
        in_specs=placed,
        out_specs=(P("rep", "shard", None), P(None, "shard", None)),
        check_vma=False,
    )
```
